1024 devices in a mesh: dp: 4 (over x), half: 4 (over y), own: 64 (over z, core).
Axes of the slice: x: 4, y: 4, z: 32, core: 2. Of those that a mesh axis runs over, the one named last changes fastest.
Arguments:
- grad_parts: bfloat16 [4, 132, 1024, 1024], P('dp', None, ('half', 'own')), may hold values from -6 to 6
- owner_table: int32 [132, 1], replicated, may hold values from 0 to 63; in each aligned block of 132 rows (0 to 131, 132 to 263, ...) at most 4 rows name the same one
- left_basis: bfloat16 [256, 1024, 1024], P(('half', 'own')), may hold values from -0.1875 to 0.1875
- right_basis: bfloat16 [256, 1024, 1024], P(('half', 'own')), may hold values from -0.1875 to 0.1875
- first_moment: bfloat16 [256, 1024, 1024], P(('half', 'own'), 'dp'), may hold values from -6 to 6
- second_moment: bfloat16 [256, 1024, 1024], P(('half', 'own'), 'dp'), may hold values from 0.5 to 8
Outputs:
- update: bfloat16 [132, 1024, 1024], P(None, ('half', 'own'), 'dp')
The draws below stay inside these ranges and needn't reach their ends.
Inputs may be any that keep to these rules, and one draw needn't show every extreme that they name: `owner_table`: every owner index is named by at least one block and by at most 4 blocks; some owner is named by exactly 4 blocks.
All inputs are finite; a program needn't handle non-finite values.
Results may differ from the reference program's by a relative error of at most 0.013.
Values may be sent and summed in bfloat16 or wider, within the bound.
No kernel may reach another device: no remote copies, remote signals or barrier semaphores. Data moves between devices by JAX's collectives and lax.ppermute only.
A program may use at most 128 MiB of HBM per device.

```python
import math
import jax
import jax.numpy as jnp
import numpy as np
from jax import lax

B = 1024
BLOCKS = 132
SLOTS = 256
N_DP = 4
N_HALF = 4
N_OWN = 64


def block_scale(rng, extent, shards, least, largest):
    def one(axis_at, parts):
        draws = jax.random.uniform(jax.random.fold_in(jax.random.fold_in(rng, 6), axis_at), (parts,), jnp.float32, least / len(shards), largest / len(shards))
        return jnp.repeat(jnp.exp(draws), extent[axis_at] // parts).reshape((-1,) + (1,) * (len(extent) - axis_at - 1))

    factor_of = one(*shards[0])
    for cut in shards[1:]:
        factor_of = factor_of * one(*cut)
    return factor_of


def shared_out(rng, own, number, rows, amount, top, limit, slope):
    sequence = jax.random.permutation(rng, amount)
    heavy_load, ordinary = shares(amount, rows * top, limit, slope, True), shares(amount, rows * top, limit, slope, False)
    places = jnp.arange(amount)

    def named(sizes, offset_by):
        used = int((sizes > 0).sum())
        fixed = max(1, used // 4)
        passed = fixed + (places - fixed + offset_by * (used - fixed)) % max(1, amount - fixed)
        return jnp.zeros((amount,), jnp.int32).at[sequence[jnp.where(places < fixed, places, passed)]].set(jnp.asarray(sizes, jnp.int32))

    sizes = jnp.where(number % 4 == 0, named(heavy_load, number // 4), named(ordinary, number - number // 4 - 1))
    mixed = jax.random.permutation(jax.random.fold_in(own, 3), amount)
    donor, sink = mixed[0:amount // 2 * 2:2], mixed[1:amount // 2 * 2:2]
    margin = jnp.minimum(sizes[donor] - 1, limit - sizes[sink]) // 2
    margin = jnp.where((donor == sequence[0]) | (sink == sequence[0]) | (sizes[sink] == 0), 0, jnp.maximum(margin, 0))
    passed = jax.random.randint(jax.random.fold_in(own, 4), (amount // 2,), 0, 1 << 20) % (margin + 1)
    sizes = sizes.at[donor].add(-passed).at[sink].add(passed)
    items = jnp.searchsorted(jnp.cumsum(sizes), jnp.arange(rows * top), side="right").astype(jnp.int32)
    grid = items.reshape(top, rows).T
    grid = grid[jax.random.permutation(jax.random.fold_in(own, 1), rows)]
    offset_by = jax.random.randint(jax.random.fold_in(own, 2), (rows, 1), 0, top)
    return jnp.take_along_axis(grid, (jnp.arange(top)[None, :] + offset_by) % top, axis=1)


def shares(count, total, reach, lean, full):
    portions = [(1 << 20) // math.isqrt(grade ** lean) + 1 for grade in range(1, count + 1)]
    largest = reach if full else min(reach, max(-(-total // count), total * portions[0] // sum(portions)))
    least = 1 if total - largest >= count - 1 else 0
    holding, surplus = [largest] + [least] * (count - 1), total - largest - least * (count - 1)
    while surplus > 0:
        candidates = [i for i in range(1, count) if holding[i] < largest] or [i for i in range(1, count) if holding[i] < reach]
        pool, budget = sum([portions[i] for i in candidates]), surplus
        for i in candidates:
            extra = min(reach - holding[i], max(1, budget * portions[i] // pool), surplus)
            holding[i] = holding[i] + extra
            surplus = surplus - extra
    return np.array(holding)


def centred(rng, extent, spread, limit, pieces=(), kind=jnp.bfloat16):
    values = jax.random.normal(rng, extent, jnp.float32) * spread
    if len(pieces) > 0:
        values = block_scale(rng, extent, pieces, -0.22, 0.18) * values
    return jnp.clip(values, min=-limit, max=limit).astype(kind)


def setup_inputs(seed: int = 0) -> dict:
    arg_keys = jax.random.split(jax.random.key(seed), 7)
    grad_parts = centred(arg_keys[0], (N_DP, BLOCKS, B, B), 1.0, 6.0, ((0, 4), (2, 256)))
    owner_table_keys = jax.random.split(jax.random.fold_in(arg_keys[1], 1), BLOCKS // BLOCKS)
    owner_table_turns = jax.random.permutation(jax.random.fold_in(arg_keys[1], 3), BLOCKS // BLOCKS)
    owner_table = jax.vmap(lambda own, number: shared_out(jax.random.fold_in(arg_keys[1], 2), own, number, BLOCKS, N_OWN, 1, N_HALF, 2))(owner_table_keys, owner_table_turns).reshape((BLOCKS, 1))
    left_basis = centred(arg_keys[2], (SLOTS, B, B), B ** -0.5, 0.1875, ((0, 256),))
    right_basis = centred(arg_keys[3], (SLOTS, B, B), B ** -0.5, 0.1875, ((0, 256),))
    first_moment = centred(arg_keys[4], (SLOTS, B, B), 1.0, 6.0, ((0, 256), (1, 4)))
    second_moment = jnp.clip(jnp.exp(math.log(8.0) - 2.7725887 * jax.random.uniform(arg_keys[5], (SLOTS, B, B), jnp.float32) ** block_scale(arg_keys[5], (SLOTS, B, B), ((0, 256), (1, 4)), -0.2, 0.2)), 0.5, 8.0).astype(jnp.bfloat16)
    return dict(grad_parts=grad_parts, owner_table=owner_table, left_basis=left_basis, right_basis=right_basis, first_moment=first_moment, second_moment=second_moment)


beta_first = 0.9
beta_second = 0.95
bias_first = 1.0 - 0.9 ** 10
bias_second = 1.0 - 0.95 ** 10
epsilon = 1e-08

def slot_numbers(owner_table):
    owner_ids = owner_table[:, 0].astype(jnp.int32)
    positions = jnp.arange(owner_ids.shape[0], dtype=jnp.int32)
    shared = (owner_ids[:, None] == owner_ids[None, :]) & (positions[None, :] < positions[:, None])
    ranking = lax.optimization_barrier(jnp.sum(shared.astype(jnp.int32), axis=1)).astype(jnp.int32)
    return (ranking * N_OWN + owner_ids).astype(jnp.int32)

def reference(grad_parts, owner_table, left_basis, right_basis, first_moment, second_moment):
    running = grad_parts[0].astype(jnp.float32)
    for replica in range(1, N_DP):
        running = running + grad_parts[replica].astype(jnp.float32)
    gradient = running.astype(jnp.bfloat16)
    slot_ids = slot_numbers(owner_table)

    def per_block(inputs):
        block_grad, slot_index = inputs
        left_matrix = left_basis[slot_index]
        right_matrix = right_basis[slot_index]
        projected = jnp.dot(left_matrix.T, block_grad, preferred_element_type=jnp.float32).astype(jnp.bfloat16)
        rotated = jnp.dot(projected, right_matrix, preferred_element_type=jnp.float32)
        first_new = beta_first * first_moment[slot_index].astype(jnp.float32) + (1.0 - beta_first) * rotated
        second_new = beta_second * second_moment[slot_index].astype(jnp.float32) + (1.0 - beta_second) * rotated * rotated
        direction = (first_new / bias_first / (jnp.sqrt(second_new / bias_second) + epsilon)).astype(jnp.bfloat16)
        back = jnp.dot(direction, right_matrix.T, preferred_element_type=jnp.float32).astype(jnp.bfloat16)
        update = jnp.dot(left_matrix, back, preferred_element_type=jnp.float32)
        return update.astype(jnp.bfloat16)
    return lax.map(per_block, (gradient, slot_ids))
```

```python
import jax
import jax.numpy as jnp
from jax import lax
from jax.sharding import Mesh, PartitionSpec as P

beta_first = 0.9
beta_second = 0.95
bias_first = 1.0 - 0.9**10
bias_second = 1.0 - 0.95**10
epsilon = 1e-08
cores = 2


def exchange(array, axes):
    return lax.all_to_all(array, axes, split_axis=0, concat_axis=0, tiled=True)


def slot_select(owner_table, owner_count, ranks):
    owner_ids = owner_table[:, 0]
    positions = jnp.arange(owner_ids.shape[0], dtype=jnp.int32)
    shared = (owner_ids[:, None] == owner_ids[None, :]) & (positions[None, :] < positions[:, None])
    ranking = jnp.sum(shared.astype(jnp.int32), axis=1)
    places = (ranking * cores + owner_ids % cores) * (owner_count // cores) + owner_ids // cores
    slot_range = jnp.arange(owner_count * ranks, dtype=jnp.int32)
    return (slot_range[:, None] == places[None, :]).astype(jnp.bfloat16)


def local(grad_parts, owner_table, left_basis, right_basis, first_moment, second_moment):
    replicas = lax.axis_size("dp")
    halves = lax.axis_size("half")
    depth = lax.axis_size("z")
    owners = depth * cores
    _, block_count, piece_rows, width = grad_parts.shape
    quarter = width // replicas
    left = left_basis[0]
    right = right_basis[0]

    parts = jnp.moveaxis(grad_parts[0].reshape(block_count, piece_rows, replicas, quarter), 2, 0)
    summed = exchange(parts, "dp").astype(jnp.float32).sum(axis=0).astype(jnp.bfloat16)

    selector = slot_select(owner_table, owners, halves)
    packed = jnp.dot(
        selector,
        summed.reshape(block_count, piece_rows * quarter),
        preferred_element_type=jnp.float32,
    ).astype(jnp.bfloat16)
    packed = packed.reshape(halves * cores, depth, piece_rows, quarter)
    arrived = exchange(packed, ("half", "core"))
    arrived = exchange(jnp.moveaxis(arrived, 1, 0), "z")
    arrived = arrived.reshape(depth, halves, cores, piece_rows, quarter)
    block = jnp.moveaxis(arrived, 1, 0).reshape(width, quarter)

    projected = lax.dot_general(
        left, block, (((0,), (0,)), ((), ())), preferred_element_type=jnp.float32
    ).astype(jnp.bfloat16)
    projected = exchange(projected.reshape(replicas, quarter, quarter), "dp")
    rotated = lax.dot_general(
        jnp.moveaxis(projected, 0, 1).reshape(quarter, width),
        right,
        (((1,), (0,)), ((), ())),
        preferred_element_type=jnp.float32,
    )
    first_new = beta_first * first_moment[0].astype(jnp.float32) + (1.0 - beta_first) * rotated
    second_new = (
        beta_second * second_moment[0].astype(jnp.float32) + (1.0 - beta_second) * rotated * rotated
    )
    direction = (first_new / bias_first / (jnp.sqrt(second_new / bias_second) + epsilon)).astype(
        jnp.bfloat16
    )
    back = lax.dot_general(
        direction, right, (((1,), (1,)), ((), ())), preferred_element_type=jnp.float32
    ).astype(jnp.bfloat16)
    back = exchange(jnp.moveaxis(back.reshape(quarter, replicas, quarter), 1, 0), "dp")
    update = jnp.dot(left, back.reshape(width, quarter), preferred_element_type=jnp.float32)

    outgoing = update.astype(jnp.bfloat16).reshape(halves, depth, cores, piece_rows, quarter)
    outgoing = jnp.moveaxis(outgoing, 1, 0).reshape(depth, halves * cores, piece_rows, quarter)
    returned = exchange(outgoing, "z")
    returned = exchange(jnp.moveaxis(returned, 1, 0), ("half", "core"))
    placed = lax.dot_general(
        selector,
        returned.reshape(halves * owners, piece_rows * quarter),
        (((0,), (0,)), ((), ())),
        preferred_element_type=jnp.float32,
    )
    return placed.astype(jnp.bfloat16).reshape(block_count, piece_rows, quarter)


def solution(mesh):
    replicas, halves, owners = (mesh.shape[axis] for axis in ("dp", "half", "own"))
    fine = Mesh(
        mesh.devices.reshape(replicas, halves, owners // cores, cores), ("dp", "half", "z", "core")
    )
    slots = ("half", "z", "core")
    return jax.shard_map(
        local,
        mesh=fine,
        in_specs=(
            P("dp", None, slots, None),
            P(),
            P(slots, None, None),
            P(slots, None, None),
            P(slots, "dp", None),
            P(slots, "dp", None),
        ),
        out_specs=P(None, slots, "dp"),
        check_vma=False,
    )
```

```python
import jax
import jax.numpy as jnp
from jax import lax
from jax.experimental import pallas as pl
from jax.experimental.pallas import tpu as pltpu
from jax.sharding import PartitionSpec as P

beta_first = 0.9
beta_second = 0.95
bias_first = 1.0 - 0.9**10
bias_second = 1.0 - 0.95**10
epsilon = 1e-08
mib = 1 << 20


def exchange(array, axes):
    return lax.all_to_all(array, axes, split_axis=0, concat_axis=0, tiled=True)


def slot_select(owner_table, owner_count, slot_count):
    owner_ids = owner_table[:, 0]
    positions = jnp.arange(owner_ids.shape[0], dtype=jnp.int32)
    shared = (owner_ids[:, None] == owner_ids[None, :]) & (positions[None, :] < positions[:, None])
    ranking = jnp.sum(shared.astype(jnp.int32), axis=1)
    slot_ids = ranking * owner_count + owner_ids
    slot_range = jnp.arange(slot_count, dtype=jnp.int32)
    return (slot_range[:, None] == slot_ids[None, :]).astype(jnp.bfloat16)


def cut_columns(array, pieces):
    blocks, rows, width = array.shape
    part = width // pieces

    def kernel(source, target, done):
        copies = [
            pltpu.make_async_copy(
                source.at[:, :, pl.ds(p * part, part)], target.at[p], done.at[p]
            )
            for p in range(pieces)
        ]
        for copy in copies:
            copy.start()
        for copy in copies:
            copy.wait()

    return pl.pallas_call(
        kernel,
        out_shape=jax.ShapeDtypeStruct((pieces, blocks, rows, part), array.dtype),
        in_specs=[pl.BlockSpec(memory_space=pl.ANY)],
        out_specs=pl.BlockSpec(memory_space=pl.ANY),
        scratch_shapes=[pltpu.SemaphoreType.DMA((pieces,))],
        compiler_params=pltpu.CompilerParams(vmem_limit_bytes=mib),
        cost_estimate=pl.CostEstimate(
            flops=0, bytes_accessed=2 * array.size * array.dtype.itemsize, transcendentals=0
        ),
    )(array)


def turned_step(projected, right, first_moment, second_moment):
    pieces, rows, part = projected.shape
    width = pieces * part

    def kernel(projected, right, first_moment, second_moment, back, direction):
        left_rows = jnp.concatenate([projected[p] for p in range(pieces)], axis=1)
        for p in range(pieces):
            columns = pl.ds(p * part, part)
            rotated = jnp.dot(left_rows, right[:, columns], preferred_element_type=jnp.float32)
            first_new = (
                beta_first * first_moment[:, columns].astype(jnp.float32)
                + (1.0 - beta_first) * rotated
            )
            second_new = (
                beta_second * second_moment[:, columns].astype(jnp.float32)
                + (1.0 - beta_second) * rotated * rotated
            )
            direction[:, columns] = (
                first_new / bias_first / (jnp.sqrt(second_new / bias_second) + epsilon)
            ).astype(jnp.bfloat16)
        for p in range(pieces):
            back[p] = lax.dot_general(
                direction[...],
                right[pl.ds(p * part, part), :],
                (((1,), (1,)), ((), ())),
                preferred_element_type=jnp.float32,
            ).astype(jnp.bfloat16)

    return pl.pallas_call(
        kernel,
        out_shape=jax.ShapeDtypeStruct((pieces, rows, part), jnp.bfloat16),
        scratch_shapes=[pltpu.VMEM((rows, width), jnp.bfloat16)],
        compiler_params=pltpu.CompilerParams(vmem_limit_bytes=24 * mib),
        cost_estimate=pl.CostEstimate(
            flops=4 * rows * width * width,
            bytes_accessed=2 * (width * width + 4 * rows * width),
            transcendentals=2 * rows * width,
        ),
    )(projected, right, first_moment, second_moment)


def local(grad_parts, owner_table, left_basis, right_basis, first_moment, second_moment):
    replicas, halves, owners = (lax.axis_size(axis) for axis in ("dp", "half", "own"))
    _, block_count, piece_rows, width = grad_parts.shape
    quarter = width // replicas
    left = left_basis[0]

    parts = exchange(cut_columns(grad_parts[0], replicas), "dp")
    summed = parts.astype(jnp.float32).sum(axis=0).astype(jnp.bfloat16)

    selector = slot_select(owner_table, owners, halves * owners)
    packed = jnp.dot(
        selector,
        summed.reshape(block_count, piece_rows * quarter),
        preferred_element_type=jnp.float32,
    ).astype(jnp.bfloat16)
    block = exchange(packed.reshape(halves * owners, piece_rows, quarter), ("half", "own"))

    projected = lax.dot_general(
        left,
        block.reshape(width, quarter),
        (((0,), (0,)), ((), ())),
        preferred_element_type=jnp.float32,
    ).astype(jnp.bfloat16)
    projected = exchange(projected.reshape(replicas, quarter, quarter), "dp")
    back = turned_step(projected, right_basis[0], first_moment[0], second_moment[0])
    back = exchange(back, "dp")
    update = jnp.dot(left, back.reshape(width, quarter), preferred_element_type=jnp.float32)

    outgoing = update.astype(jnp.bfloat16).reshape(halves * owners, piece_rows, quarter)
    returned = exchange(outgoing, ("half", "own"))
    placed = lax.dot_general(
        selector,
        returned.reshape(halves * owners, piece_rows * quarter),
        (((0,), (0,)), ((), ())),
        preferred_element_type=jnp.float32,
    )
    return placed.astype(jnp.bfloat16).reshape(block_count, piece_rows, quarter)


def solution(mesh):
    slots = ("half", "own")
    return jax.shard_map(
        local,
        mesh=mesh,
        in_specs=(
            P("dp", None, slots, None),
            P(),
            P(slots, None, None),
            P(slots, None, None),
            P(slots, "dp", None),
            P(slots, "dp", None),
        ),
        out_specs=P(None, slots, "dp"),
        check_vma=False,
    )
```

```python
import jax
import jax.numpy as jnp
from jax import lax
from jax.experimental import pallas as pl
from jax.experimental.pallas import tpu as pltpu
from jax.sharding import PartitionSpec as P

beta_first = 0.9
beta_second = 0.95
bias_first = 1.0 - 0.9**10
bias_second = 1.0 - 0.95**10
epsilon = 1e-08
mib = 1 << 20


def in_hbm(array):
    return pltpu.with_memory_space_constraint(array, pltpu.HBM)


def exchange(array, axes):
    return lax.all_to_all(array, axes, split_axis=0, concat_axis=0, tiled=True)


def slot_numbers(owner_table, owner_count):
    owner_ids = owner_table[:, 0]
    positions = jnp.arange(owner_ids.shape[0], dtype=jnp.int32)
    shared = (owner_ids[:, None] == owner_ids[None, :]) & (positions[None, :] < positions[:, None])
    ranking = jnp.sum(shared.astype(jnp.int32), axis=1)
    return ranking * owner_count + owner_ids


def cut_columns(array, pieces):
    blocks, rows, width = array.shape
    part = width // pieces

    def kernel(source, target, done):
        copies = [
            pltpu.make_async_copy(
                source.at[:, :, pl.ds(p * part, part)], target.at[p], done.at[p]
            )
            for p in range(pieces)
        ]
        for copy in copies:
            copy.start()
        for copy in copies:
            copy.wait()

    return pl.pallas_call(
        kernel,
        out_shape=jax.ShapeDtypeStruct((pieces, blocks, rows, part), array.dtype),
        in_specs=[pl.BlockSpec(memory_space=pltpu.HBM)],
        out_specs=pl.BlockSpec(memory_space=pltpu.HBM),
        scratch_shapes=[pltpu.SemaphoreType.DMA((pieces,))],
        compiler_params=pltpu.CompilerParams(vmem_limit_bytes=mib),
        cost_estimate=pl.CostEstimate(
            flops=0, bytes_accessed=2 * array.size * array.dtype.itemsize, transcendentals=0
        ),
    )(in_hbm(array))


def projected_columns(block, left, pieces):
    width, columns = block.shape
    part = width // pieces

    def kernel(block, left, out):
        for p in range(pieces):
            out[p] = lax.dot_general(
                block[...],
                left[:, pl.ds(p * part, part)],
                (((0,), (0,)), ((), ())),
                preferred_element_type=jnp.float32,
            ).astype(jnp.bfloat16)

    return pl.pallas_call(
        kernel,
        out_shape=jax.ShapeDtypeStruct((pieces, columns, part), jnp.bfloat16),
        compiler_params=pltpu.CompilerParams(vmem_limit_bytes=16 * mib),
        cost_estimate=pl.CostEstimate(
            flops=2 * width * width * columns,
            bytes_accessed=2 * (width * width + 2 * width * columns),
            transcendentals=0,
        ),
    )(block, left)


def turned_step(projected, right, first_moment, second_moment):
    pieces, part, rows = projected.shape
    width = pieces * part

    def kernel(projected, right, first, second, back, right_held, first_held, second_held, direction, done):
        cuts = [pl.ds(p * part, part) for p in range(pieces)]
        pairs = ((right, right_held), (first, first_held), (second, second_held))
        copies = [
            [
                pltpu.make_async_copy(source.at[:, cut], target.at[:, cut], done.at[n, p])
                for n, (source, target) in enumerate(pairs)
            ]
            for p, cut in enumerate(cuts)
        ]
        for group in copies:
            for copy in group:
                copy.start()
        turned = projected[...].reshape(width, rows)
        for cut, group in zip(cuts, copies):
            for copy in group:
                copy.wait()
            rotated = lax.dot_general(
                turned,
                right_held[:, cut],
                (((0,), (0,)), ((), ())),
                preferred_element_type=jnp.float32,
            )
            first_new = (
                beta_first * first_held[:, cut].astype(jnp.float32) + (1.0 - beta_first) * rotated
            )
            second_new = (
                beta_second * second_held[:, cut].astype(jnp.float32)
                + (1.0 - beta_second) * rotated * rotated
            )
            direction[:, cut] = (
                first_new / bias_first / (jnp.sqrt(second_new / bias_second) + epsilon)
            ).astype(jnp.bfloat16)
        for p, cut in enumerate(cuts):
            back[p] = lax.dot_general(
                direction[...],
                right_held[cut, :],
                (((1,), (1,)), ((), ())),
                preferred_element_type=jnp.float32,
            ).astype(jnp.bfloat16)

    here, far = pl.BlockSpec(memory_space=pltpu.VMEM), pl.BlockSpec(memory_space=pltpu.HBM)
    return pl.pallas_call(
        kernel,
        out_shape=jax.ShapeDtypeStruct((pieces, rows, part), jnp.bfloat16),
        in_specs=[here, far, far, far],
        out_specs=here,
        scratch_shapes=[
            pltpu.VMEM((width, width), jnp.bfloat16),
            pltpu.VMEM((rows, width), jnp.bfloat16),
            pltpu.VMEM((rows, width), jnp.bfloat16),
            pltpu.VMEM((rows, width), jnp.bfloat16),
            pltpu.SemaphoreType.DMA((3, pieces)),
        ],
        compiler_params=pltpu.CompilerParams(vmem_limit_bytes=16 * mib),
        cost_estimate=pl.CostEstimate(
            flops=4 * rows * width * width,
            bytes_accessed=2 * (width * width + 4 * rows * width),
            transcendentals=2 * rows * width,
        ),
    )(projected, *(in_hbm(array) for array in (right, first_moment, second_moment)))


def taken(array, places):
    count = places.shape[0]
    shape = (count, *array.shape[1:])

    def kernel(places, source, target):
        def one(b, carry):
            target[b] = source[places[b]]
            return carry

        lax.fori_loop(0, count, one, 0, unroll=4)

    here = pl.BlockSpec(memory_space=pltpu.VMEM)
    return pl.pallas_call(
        kernel,
        out_shape=jax.ShapeDtypeStruct(shape, array.dtype),
        in_specs=[pl.BlockSpec(memory_space=pltpu.SMEM), here],
        out_specs=here,
        compiler_params=pltpu.CompilerParams(vmem_limit_bytes=8 * mib),
        cost_estimate=pl.CostEstimate(
            flops=0,
            bytes_accessed=2 * array.size * array.dtype.itemsize,
            transcendentals=0,
        ),
    )(places, array)


def local(grad_parts, owner_table, left_basis, right_basis, first_moment, second_moment):
    replicas, halves, owners = (lax.axis_size(axis) for axis in ("dp", "half", "own"))
    _, block_count, piece_rows, width = grad_parts.shape
    quarter = width // replicas
    left = left_basis[0]

    parts = exchange(cut_columns(grad_parts[0], replicas), "dp")
    summed = parts.astype(jnp.float32).sum(axis=0).astype(jnp.bfloat16)

    slot_ids = slot_numbers(owner_table, owners)
    slot_range = jnp.arange(halves * owners, dtype=jnp.int32)
    selector = (slot_range[:, None] == slot_ids[None, :]).astype(jnp.bfloat16)
    packed = jnp.dot(
        selector,
        summed.reshape(block_count, piece_rows * quarter),
        preferred_element_type=jnp.float32,
    ).astype(jnp.bfloat16)
    block = exchange(packed.reshape(halves * owners, piece_rows, quarter), ("half", "own"))

    projected = exchange(
        projected_columns(block.reshape(width, quarter), left, replicas), "dp"
    )
    back = turned_step(projected, right_basis[0], first_moment[0], second_moment[0])
    back = exchange(back, "dp")
    update = jnp.dot(left, back.reshape(width, quarter), preferred_element_type=jnp.float32)

    outgoing = update.astype(jnp.bfloat16).reshape(halves * owners, piece_rows, quarter)
    returned = exchange(outgoing, ("half", "own"))
    return taken(returned, slot_ids)


def solution(mesh):
    slots = ("half", "own")
    return jax.shard_map(
        local,
        mesh=mesh,
        in_specs=(
            P("dp", None, slots, None),
            P(),
            P(slots, None, None),
            P(slots, None, None),
            P(slots, "dp", None),
            P(slots, "dp", None),
        ),
        out_specs=P(None, slots, "dp"),
        check_vma=False,
    )
```

```python
import jax
import jax.numpy as jnp
from jax import lax
from jax.experimental import pallas as pl
from jax.experimental.pallas import tpu as pltpu
from jax.sharding import PartitionSpec as P

beta_first = 0.9
beta_second = 0.95
bias_first = 1.0 - 0.9**10
bias_second = 1.0 - 0.95**10
epsilon = 1e-08
mib = 1 << 20


def in_hbm(array):
    return pltpu.with_memory_space_constraint(array, pltpu.HBM)


def exchange(array, axes):
    return lax.all_to_all(array, axes, split_axis=0, concat_axis=0, tiled=True)


def slot_numbers(owner_table, owner_count):
    owner_ids = owner_table[:, 0]
    positions = jnp.arange(owner_ids.shape[0], dtype=jnp.int32)
    shared = (owner_ids[:, None] == owner_ids[None, :]) & (positions[None, :] < positions[:, None])
    ranking = jnp.sum(shared.astype(jnp.int32), axis=1)
    return ranking * owner_count + owner_ids


def cut_columns(array, pieces):
    blocks, rows, width = array.shape
    part = width // pieces

    def kernel(source, target, done):
        copies = [
            pltpu.make_async_copy(
                source.at[:, :, pl.ds(p * part, part)], target.at[p], done.at[p]
            )
            for p in range(pieces)
        ]
        for copy in copies:
            copy.start()
        for copy in copies:
            copy.wait()

    return pl.pallas_call(
        kernel,
        out_shape=pltpu.VMEM((pieces, blocks, rows, part), array.dtype),
        in_specs=[pl.BlockSpec(memory_space=pltpu.HBM)],
        out_specs=pl.BlockSpec(memory_space=pltpu.VMEM),
        scratch_shapes=[pltpu.SemaphoreType.DMA((pieces,))],
        compiler_params=pltpu.CompilerParams(vmem_limit_bytes=8 * mib),
        cost_estimate=pl.CostEstimate(
            flops=0, bytes_accessed=2 * array.size * array.dtype.itemsize, transcendentals=0
        ),
    )(in_hbm(array))


def projected_columns(block, left, pieces):
    width, columns = block.shape
    part = width // pieces

    def kernel(block, left, out):
        for p in range(pieces):
            out[p] = lax.dot_general(
                block[...],
                left[:, pl.ds(p * part, part)],
                (((0,), (0,)), ((), ())),
                preferred_element_type=jnp.float32,
            ).astype(jnp.bfloat16)

    return pl.pallas_call(
        kernel,
        out_shape=jax.ShapeDtypeStruct((pieces, columns, part), jnp.bfloat16),
        compiler_params=pltpu.CompilerParams(vmem_limit_bytes=16 * mib),
        cost_estimate=pl.CostEstimate(
            flops=2 * width * width * columns,
            bytes_accessed=2 * (width * width + 2 * width * columns),
            transcendentals=0,
        ),
    )(block, left)


def turned_step(projected, right, first_moment, second_moment):
    pieces, part, rows = projected.shape
    width = pieces * part

    def kernel(projected, right, first, second, back, direction):
        turned = projected[...].reshape(width, rows)
        cuts = [pl.ds(p * part, part) for p in range(pieces)]
        for cut in cuts:
            rotated = lax.dot_general(
                turned,
                right[:, cut],
                (((0,), (0,)), ((), ())),
                preferred_element_type=jnp.float32,
            )
            first_new = (
                beta_first * first[:, cut].astype(jnp.float32) + (1.0 - beta_first) * rotated
            )
            second_new = (
                beta_second * second[:, cut].astype(jnp.float32)
                + (1.0 - beta_second) * rotated * rotated
            )
            direction[:, cut] = (
                first_new / bias_first / (jnp.sqrt(second_new / bias_second) + epsilon)
            ).astype(jnp.bfloat16)
        for p, cut in enumerate(cuts):
            back[p] = lax.dot_general(
                direction[...],
                right[cut, :],
                (((1,), (1,)), ((), ())),
                preferred_element_type=jnp.float32,
            ).astype(jnp.bfloat16)

    return pl.pallas_call(
        kernel,
        out_shape=jax.ShapeDtypeStruct((pieces, rows, part), jnp.bfloat16),
        scratch_shapes=[pltpu.VMEM((rows, width), jnp.bfloat16)],
        compiler_params=pltpu.CompilerParams(vmem_limit_bytes=16 * mib),
        cost_estimate=pl.CostEstimate(
            flops=4 * rows * width * width,
            bytes_accessed=2 * (width * width + 4 * rows * width),
            transcendentals=2 * rows * width,
        ),
    )(projected, right, first_moment, second_moment)


def product(left, right):
    def kernel(left, right, out):
        out[...] = jnp.dot(
            left[...], right[...], preferred_element_type=jnp.float32
        ).astype(jnp.bfloat16)

    rows, inner = left.shape
    columns = right.shape[1]
    return pl.pallas_call(
        kernel,
        out_shape=jax.ShapeDtypeStruct((rows, columns), jnp.bfloat16),
        compiler_params=pltpu.CompilerParams(vmem_limit_bytes=16 * mib),
        cost_estimate=pl.CostEstimate(
            flops=2 * rows * inner * columns,
            bytes_accessed=2 * (rows * inner + inner * columns + rows * columns),
            transcendentals=0,
        ),
    )(left, right)


def taken(array, places):
    count = places.shape[0]
    shape = (count, *array.shape[1:])

    def kernel(places, source, target):
        def one(b, carry):
            target[b] = source[places[b]]
            return carry

        lax.fori_loop(0, count, one, 0, unroll=12)

    here = pl.BlockSpec(memory_space=pltpu.VMEM)
    return pl.pallas_call(
        kernel,
        out_shape=jax.ShapeDtypeStruct(shape, array.dtype),
        in_specs=[pl.BlockSpec(memory_space=pltpu.SMEM), here],
        out_specs=here,
        compiler_params=pltpu.CompilerParams(vmem_limit_bytes=8 * mib),
        cost_estimate=pl.CostEstimate(
            flops=0,
            bytes_accessed=2 * array.size * array.dtype.itemsize,
            transcendentals=0,
        ),
    )(places, array)


def local(grad_parts, owner_table, left_basis, right_basis, first_moment, second_moment):
    replicas, halves, owners = (lax.axis_size(axis) for axis in ("dp", "half", "own"))
    _, block_count, piece_rows, width = grad_parts.shape
    quarter = width // replicas
    left = left_basis[0]

    parts = exchange(cut_columns(grad_parts[0], replicas), "dp")
    summed = parts.astype(jnp.float32).sum(axis=0).astype(jnp.bfloat16)

    slot_ids = slot_numbers(owner_table, owners)
    slot_range = jnp.arange(halves * owners, dtype=jnp.int32)
    selector = (slot_range[:, None] == slot_ids[None, :]).astype(jnp.bfloat16)
    packed = jnp.dot(
        selector,
        summed.reshape(block_count, piece_rows * quarter),
        preferred_element_type=jnp.float32,
    ).astype(jnp.bfloat16)
    block = exchange(packed.reshape(halves * owners, piece_rows, quarter), ("half", "own"))

    projected = exchange(
        projected_columns(block.reshape(width, quarter), left, replicas), "dp"
    )
    back = turned_step(projected, right_basis[0], first_moment[0], second_moment[0])
    back = exchange(back, "dp")
    update = product(left, back.reshape(width, quarter))

    outgoing = update.reshape(halves * owners, piece_rows, quarter)
    returned = exchange(outgoing, ("half", "own"))
    return taken(returned, slot_ids)


def solution(mesh):
    slots = ("half", "own")
    return jax.shard_map(
        local,
        mesh=mesh,
        in_specs=(
            P("dp", None, slots, None),
            P(),
            P(slots, None, None),
            P(slots, None, None),
            P(slots, "dp", None),
            P(slots, "dp", None),
        ),
        out_specs=P(None, slots, "dp"),
        check_vma=False,
    )
```

```python
import jax
import jax.numpy as jnp
from jax import lax
from jax.experimental import pallas as pl
from jax.experimental.pallas import tpu as pltpu
from jax.sharding import Mesh, PartitionSpec as P

beta_first = 0.9
beta_second = 0.95
bias_first = 1.0 - 0.9**10
bias_second = 1.0 - 0.95**10
epsilon = 1e-08
mib = 1 << 20
cores = 2


def in_hbm(array):
    return pltpu.with_memory_space_constraint(array, pltpu.HBM)


def exchange(array, axes):
    return lax.all_to_all(array, axes, split_axis=0, concat_axis=0, tiled=True)


def slot_places(owner_table, ranks, depth):
    owner_ids = owner_table[:, 0]
    positions = jnp.arange(owner_ids.shape[0], dtype=jnp.int32)
    shared = (owner_ids[:, None] == owner_ids[None, :]) & (positions[None, :] < positions[:, None])
    ranking = jnp.sum(shared.astype(jnp.int32), axis=1)
    return ((owner_ids % cores) * ranks + ranking) * depth + owner_ids // cores


def in_turn(array, depth):
    away = depth * 3 // 8
    pairs = [(z * cores + 1, (z + away) % depth * cores + 1) for z in range(depth)]
    turn = lax.ppermute(array[0, 0], ("z", "core"), pairs)
    return lax.optimization_barrier((array, turn))


def cut_columns(array, pieces):
    blocks, rows, width = array.shape
    part = width // pieces

    def kernel(source, target, done):
        copies = [
            pltpu.make_async_copy(
                source.at[:, :, pl.ds(p * part, part)], target.at[p], done.at[p]
            )
            for p in range(pieces)
        ]
        for copy in copies:
            copy.start()
        for copy in copies:
            copy.wait()

    return pl.pallas_call(
        kernel,
        out_shape=pltpu.VMEM((pieces, blocks, rows, part), array.dtype),
        in_specs=[pl.BlockSpec(memory_space=pltpu.HBM)],
        out_specs=pl.BlockSpec(memory_space=pltpu.VMEM),
        scratch_shapes=[pltpu.SemaphoreType.DMA((pieces,))],
        compiler_params=pltpu.CompilerParams(vmem_limit_bytes=8 * mib),
        cost_estimate=pl.CostEstimate(
            flops=0, bytes_accessed=2 * array.size * array.dtype.itemsize, transcendentals=0
        ),
    )(in_hbm(array))


def projected_columns(block, left, pieces, after):
    width, columns = block.shape
    part = width // pieces

    def kernel(block, left, after, out):
        for p in range(pieces):
            out[p] = lax.dot_general(
                block[...],
                left[:, pl.ds(p * part, part)],
                (((0,), (0,)), ((), ())),
                preferred_element_type=jnp.float32,
            ).astype(jnp.bfloat16)

    return pl.pallas_call(
        kernel,
        out_shape=jax.ShapeDtypeStruct((pieces, columns, part), jnp.bfloat16),
        in_specs=[pl.BlockSpec(memory_space=space) for space in (pltpu.VMEM, pltpu.VMEM, pl.ANY)],
        compiler_params=pltpu.CompilerParams(vmem_limit_bytes=16 * mib),
        cost_estimate=pl.CostEstimate(
            flops=2 * width * width * columns,
            bytes_accessed=2 * (width * width + 2 * width * columns),
            transcendentals=0,
        ),
    )(block, left, after)


def turned_step(projected, right, first_moment, second_moment):
    pieces, part, rows = projected.shape
    width = pieces * part

    def kernel(projected, right, first, second, back, direction):
        turned = projected[...].reshape(width, rows)
        cuts = [pl.ds(p * part, part) for p in range(pieces)]
        for cut in cuts:
            rotated = lax.dot_general(
                turned,
                right[:, cut],
                (((0,), (0,)), ((), ())),
                preferred_element_type=jnp.float32,
            )
            first_new = (
                beta_first * first[:, cut].astype(jnp.float32) + (1.0 - beta_first) * rotated
            )
            second_new = (
                beta_second * second[:, cut].astype(jnp.float32)
                + (1.0 - beta_second) * rotated * rotated
            )
            direction[:, cut] = (
                first_new / bias_first / (jnp.sqrt(second_new / bias_second) + epsilon)
            ).astype(jnp.bfloat16)
        for p, cut in enumerate(cuts):
            back[p] = lax.dot_general(
                direction[...],
                right[cut, :],
                (((1,), (1,)), ((), ())),
                preferred_element_type=jnp.float32,
            ).astype(jnp.bfloat16)

    return pl.pallas_call(
        kernel,
        out_shape=jax.ShapeDtypeStruct((pieces, rows, part), jnp.bfloat16),
        scratch_shapes=[pltpu.VMEM((rows, width), jnp.bfloat16)],
        compiler_params=pltpu.CompilerParams(vmem_limit_bytes=16 * mib),
        cost_estimate=pl.CostEstimate(
            flops=4 * rows * width * width,
            bytes_accessed=2 * (width * width + 4 * rows * width),
            transcendentals=2 * rows * width,
        ),
    )(projected, right, first_moment, second_moment)


def product(left, right):
    def kernel(left, right, out):
        out[...] = jnp.dot(
            left[...], right[...], preferred_element_type=jnp.float32
        ).astype(jnp.bfloat16)

    rows, inner = left.shape
    columns = right.shape[1]
    return pl.pallas_call(
        kernel,
        out_shape=jax.ShapeDtypeStruct((rows, columns), jnp.bfloat16),
        compiler_params=pltpu.CompilerParams(vmem_limit_bytes=16 * mib),
        cost_estimate=pl.CostEstimate(
            flops=2 * rows * inner * columns,
            bytes_accessed=2 * (rows * inner + inner * columns + rows * columns),
            transcendentals=0,
        ),
    )(left, right)


def taken(array, places):
    count = places.shape[0]
    shape = (count, *array.shape[1:])

    def kernel(places, source, target):
        def one(b, carry):
            target[b] = source[places[b]]
            return carry

        lax.fori_loop(0, count, one, 0, unroll=12)

    here = pl.BlockSpec(memory_space=pltpu.VMEM)
    return pl.pallas_call(
        kernel,
        out_shape=jax.ShapeDtypeStruct(shape, array.dtype),
        in_specs=[pl.BlockSpec(memory_space=pltpu.SMEM), here],
        out_specs=here,
        compiler_params=pltpu.CompilerParams(vmem_limit_bytes=8 * mib),
        cost_estimate=pl.CostEstimate(
            flops=0,
            bytes_accessed=2 * array.size * array.dtype.itemsize,
            transcendentals=0,
        ),
    )(places, array)


def local(grad_parts, owner_table, left_basis, right_basis, first_moment, second_moment):
    replicas, halves, depth = (lax.axis_size(axis) for axis in ("dp", "half", "z"))
    slots = halves * depth
    _, block_count, piece_rows, width = grad_parts.shape
    quarter = width // replicas
    left = left_basis[0]

    parts = exchange(cut_columns(grad_parts[0], replicas), "dp")
    summed = parts.astype(jnp.float32).sum(axis=0).astype(jnp.bfloat16)

    places = slot_places(owner_table, halves, depth)
    selector = (jnp.arange(cores * slots, dtype=jnp.int32)[:, None] == places[None, :]).astype(
        jnp.bfloat16
    )
    packed = jnp.dot(
        selector,
        summed.reshape(block_count, piece_rows * quarter),
        preferred_element_type=jnp.float32,
    ).astype(jnp.bfloat16)
    arrived = exchange(packed.reshape(cores, slots, piece_rows, quarter), "core")
    arrived, turn = in_turn(jnp.moveaxis(arrived, 1, 0), depth)
    block = exchange(arrived, ("half", "z"))

    projected = exchange(
        projected_columns(block.reshape(width, quarter), left, replicas, turn), "dp"
    )
    back = turned_step(projected, right_basis[0], first_moment[0], second_moment[0])
    back = exchange(back, "dp")
    update = product(left, back.reshape(width, quarter))

    returned = exchange(update.reshape(slots, cores, piece_rows, quarter), ("half", "z"))
    returned = exchange(jnp.moveaxis(returned, 1, 0), "core")
    return taken(returned.reshape(cores * slots, piece_rows, quarter), places)


def solution(mesh):
    replicas, halves, owners = (mesh.shape[axis] for axis in ("dp", "half", "own"))
    fine = Mesh(
        mesh.devices.reshape(replicas, halves, owners // cores, cores), ("dp", "half", "z", "core")
    )
    slots = ("half", "z", "core")
    return jax.shard_map(
        local,
        mesh=fine,
        in_specs=(
            P("dp", None, slots, None),
            P(),
            P(slots, None, None),
            P(slots, None, None),
            P(slots, "dp", None),
            P(slots, "dp", None),
        ),
        out_specs=P(None, slots, "dp"),
        check_vma=False,
    )
```

```python
import jax
import jax.numpy as jnp
from jax import lax
from jax.experimental import pallas as pl
from jax.experimental.pallas import tpu as pltpu
from jax.sharding import Mesh, PartitionSpec as P

beta_first = 0.9
beta_second = 0.95
bias_first = 1.0 - 0.9**10
bias_second = 1.0 - 0.95**10
epsilon = 1e-08
mib = 1 << 20
cores = 2


def in_hbm(array):
    return pltpu.with_memory_space_constraint(array, pltpu.HBM)


def exchange(array, axes):
    return lax.all_to_all(array, axes, split_axis=0, concat_axis=0, tiled=True)


def slot_places(owner_table, ranks, depth):
    owner_ids = owner_table[:, 0]
    positions = jnp.arange(owner_ids.shape[0], dtype=jnp.int32)
    shared = (owner_ids[:, None] == owner_ids[None, :]) & (positions[None, :] < positions[:, None])
    ranking = jnp.sum(shared.astype(jnp.int32), axis=1)
    return ((owner_ids % cores) * ranks + ranking) * depth + owner_ids // cores


def in_turn(array, depth):
    away = depth // 2
    pairs = [(z * cores + 1, (z + away) % depth * cores + 1) for z in range(depth)]
    turn = lax.ppermute(array[0, 0], ("z", "core"), pairs)
    return lax.optimization_barrier((array, turn))


def cut_columns(array, pieces):
    blocks, rows, width = array.shape
    part = width // pieces

    def kernel(source, target, done):
        copies = [
            pltpu.make_async_copy(
                source.at[:, :, pl.ds(p * part, part)], target.at[p], done.at[p]
            )
            for p in range(pieces)
        ]
        for copy in copies:
            copy.start()
        for copy in copies:
            copy.wait()

    return pl.pallas_call(
        kernel,
        out_shape=pltpu.VMEM((pieces, blocks, rows, part), array.dtype),
        in_specs=[pl.BlockSpec(memory_space=pltpu.HBM)],
        out_specs=pl.BlockSpec(memory_space=pltpu.VMEM),
        scratch_shapes=[pltpu.SemaphoreType.DMA((pieces,))],
        compiler_params=pltpu.CompilerParams(vmem_limit_bytes=8 * mib),
        cost_estimate=pl.CostEstimate(
            flops=0, bytes_accessed=2 * array.size * array.dtype.itemsize, transcendentals=0
        ),
    )(in_hbm(array))


def projected_columns(block, left, pieces, after):
    width, columns = block.shape
    part = width // pieces

    def kernel(block, left, after, out):
        for p in range(pieces):
            out[p] = lax.dot_general(
                block[...],
                left[:, pl.ds(p * part, part)],
                (((0,), (0,)), ((), ())),
                preferred_element_type=jnp.float32,
            ).astype(jnp.bfloat16)

    return pl.pallas_call(
        kernel,
        out_shape=jax.ShapeDtypeStruct((pieces, columns, part), jnp.bfloat16),
        in_specs=[pl.BlockSpec(memory_space=space) for space in (pltpu.VMEM, pltpu.VMEM, pl.ANY)],
        compiler_params=pltpu.CompilerParams(vmem_limit_bytes=16 * mib),
        cost_estimate=pl.CostEstimate(
            flops=2 * width * width * columns,
            bytes_accessed=2 * (width * width + 2 * width * columns),
            transcendentals=0,
        ),
    )(block, left, after)


def turned_step(projected, right, first_moment, second_moment):
    pieces, part, rows = projected.shape
    width = pieces * part

    def kernel(projected, right, first, second, back, direction):
        turned = projected[...].reshape(width, rows)
        cuts = [pl.ds(p * part, part) for p in range(pieces)]
        for cut in cuts:
            rotated = lax.dot_general(
                turned,
                right[:, cut],
                (((0,), (0,)), ((), ())),
                preferred_element_type=jnp.float32,
            )
            first_new = (
                beta_first * first[:, cut].astype(jnp.float32) + (1.0 - beta_first) * rotated
            )
            second_new = (
                beta_second * second[:, cut].astype(jnp.float32)
                + (1.0 - beta_second) * rotated * rotated
            )
            direction[:, cut] = (
                first_new / bias_first / (jnp.sqrt(second_new / bias_second) + epsilon)
            ).astype(jnp.bfloat16)
        for p, cut in enumerate(cuts):
            back[p] = lax.dot_general(
                direction[...],
                right[cut, :],
                (((1,), (1,)), ((), ())),
                preferred_element_type=jnp.float32,
            ).astype(jnp.bfloat16)

    return pl.pallas_call(
        kernel,
        out_shape=jax.ShapeDtypeStruct((pieces, rows, part), jnp.bfloat16),
        scratch_shapes=[pltpu.VMEM((rows, width), jnp.bfloat16)],
        compiler_params=pltpu.CompilerParams(vmem_limit_bytes=16 * mib),
        cost_estimate=pl.CostEstimate(
            flops=4 * rows * width * width,
            bytes_accessed=2 * (width * width + 4 * rows * width),
            transcendentals=2 * rows * width,
        ),
    )(projected, right, first_moment, second_moment)


def product(left, right):
    def kernel(left, right, out):
        out[...] = jnp.dot(
            left[...], right[...], preferred_element_type=jnp.float32
        ).astype(jnp.bfloat16)

    rows, inner = left.shape
    columns = right.shape[1]
    return pl.pallas_call(
        kernel,
        out_shape=jax.ShapeDtypeStruct((rows, columns), jnp.bfloat16),
        compiler_params=pltpu.CompilerParams(vmem_limit_bytes=16 * mib),
        cost_estimate=pl.CostEstimate(
            flops=2 * rows * inner * columns,
            bytes_accessed=2 * (rows * inner + inner * columns + rows * columns),
            transcendentals=0,
        ),
    )(left, right)


def taken(array, places):
    count = places.shape[0]
    shape = (count, *array.shape[1:])

    batch = max(n for n in range(1, 13) if count % n == 0)

    def kernel(places, source, target):
        def some(step, carry):
            first = step * batch
            rows = [source[places[first + n]] for n in range(batch)]
            for n, row in enumerate(rows):
                target[first + n] = row
            return carry

        lax.fori_loop(0, count // batch, some, 0)

    here = pl.BlockSpec(memory_space=pltpu.VMEM)
    return pl.pallas_call(
        kernel,
        out_shape=jax.ShapeDtypeStruct(shape, array.dtype),
        in_specs=[pl.BlockSpec(memory_space=pltpu.SMEM), here],
        out_specs=here,
        compiler_params=pltpu.CompilerParams(vmem_limit_bytes=8 * mib),
        cost_estimate=pl.CostEstimate(
            flops=0,
            bytes_accessed=2 * array.size * array.dtype.itemsize,
            transcendentals=0,
        ),
    )(places, array)


def local(grad_parts, owner_table, left_basis, right_basis, first_moment, second_moment):
    replicas, halves, depth = (lax.axis_size(axis) for axis in ("dp", "half", "z"))
    slots = halves * depth
    _, block_count, piece_rows, width = grad_parts.shape
    quarter = width // replicas
    left = left_basis[0]

    parts = exchange(cut_columns(grad_parts[0], replicas), "dp")
    summed = parts.astype(jnp.float32).sum(axis=0).astype(jnp.bfloat16)

    places = slot_places(owner_table, halves, depth)
    selector = (jnp.arange(cores * slots, dtype=jnp.int32)[:, None] == places[None, :]).astype(
        jnp.bfloat16
    )
    packed = jnp.dot(
        selector,
        summed.reshape(block_count, piece_rows * quarter),
        preferred_element_type=jnp.float32,
    ).astype(jnp.bfloat16)
    arrived = exchange(packed.reshape(cores, slots, piece_rows, quarter), "core")
    arrived, turn = in_turn(jnp.moveaxis(arrived, 1, 0), depth)
    block = exchange(arrived, ("half", "z"))

    projected = exchange(
        projected_columns(block.reshape(width, quarter), left, replicas, turn), "dp"
    )
    back = turned_step(projected, right_basis[0], first_moment[0], second_moment[0])
    back = exchange(back, "dp")
    update = product(left, back.reshape(width, quarter))

    returned = exchange(update.reshape(slots, cores, piece_rows, quarter), ("half", "z"))
    returned = exchange(jnp.moveaxis(returned, 1, 0), "core")
    return taken(returned.reshape(cores * slots, piece_rows, quarter), places)


def solution(mesh):
    replicas, halves, owners = (mesh.shape[axis] for axis in ("dp", "half", "own"))
    fine = Mesh(
        mesh.devices.reshape(replicas, halves, owners // cores, cores), ("dp", "half", "z", "core")
    )
    slots = ("half", "z", "core")
    return jax.shard_map(
        local,
        mesh=fine,
        in_specs=(
            P("dp", None, slots, None),
            P(),
            P(slots, None, None),
            P(slots, None, None),
            P(slots, "dp", None),
            P(slots, "dp", None),
        ),
        out_specs=P(None, slots, "dp"),
        check_vma=False,
    )
```

```python
import jax
import jax.numpy as jnp
from jax import lax
from jax.experimental import pallas as pl
from jax.experimental.pallas import tpu as pltpu
from jax.sharding import Mesh, PartitionSpec as P

beta_first = 0.9
beta_second = 0.95
bias_first = 1.0 - 0.9**10
bias_second = 1.0 - 0.95**10
epsilon = 1e-08
mib = 1 << 20
cores = 2


def in_hbm(array):
    return pltpu.with_memory_space_constraint(array, pltpu.HBM)


def exchange(array, axes):
    return lax.all_to_all(array, axes, split_axis=0, concat_axis=0, tiled=True)


def slot_places(owner_table, ranks, depth):
    owner_ids = owner_table[:, 0]
    positions = jnp.arange(owner_ids.shape[0], dtype=jnp.int32)
    shared = (owner_ids[:, None] == owner_ids[None, :]) & (positions[None, :] < positions[:, None])
    ranking = jnp.sum(shared.astype(jnp.int32), axis=1)
    return ((owner_ids % cores) * ranks + ranking) * depth + owner_ids // cores


def in_turn(array, depth):
    away = depth // 2
    pairs = [(z * cores + 1, (z + away) % depth * cores + 1) for z in range(depth)]
    turn = lax.ppermute(array[0, 0], ("z", "core"), pairs)
    return lax.optimization_barrier((array, turn))


def cut_columns(array, pieces):
    blocks, rows, width = array.shape
    part = width // pieces

    steps = max(n for n in range(1, 5) if blocks % n == 0)
    some = blocks // steps

    def kernel(source, target, held, came, went):
        def arrival(n):
            return pltpu.make_async_copy(
                source.at[pl.ds(n * some, some)], held.at[pl.ds(n * some, some)], came.at[n]
            )

        def departure(n, p):
            return pltpu.make_async_copy(
                held.at[pl.ds(n * some, some), :, pl.ds(p * part, part)],
                target.at[p, pl.ds(n * some, some)],
                went.at[n, p],
            )

        for n in range(steps):
            arrival(n).start()
        for n in range(steps):
            arrival(n).wait()
            for p in range(pieces):
                departure(n, p).start()
        for n in range(steps):
            for p in range(pieces):
                departure(n, p).wait()

    return pl.pallas_call(
        kernel,
        out_shape=jax.ShapeDtypeStruct((pieces, blocks, rows, part), array.dtype),
        in_specs=[pl.BlockSpec(memory_space=pltpu.HBM)],
        out_specs=pl.BlockSpec(memory_space=pl.ANY),
        scratch_shapes=[
            pltpu.VMEM(array.shape, array.dtype),
            pltpu.SemaphoreType.DMA((steps,)),
            pltpu.SemaphoreType.DMA((steps, pieces)),
        ],
        compiler_params=pltpu.CompilerParams(vmem_limit_bytes=8 * mib),
        cost_estimate=pl.CostEstimate(
            flops=0, bytes_accessed=2 * array.size * array.dtype.itemsize, transcendentals=0
        ),
    )(in_hbm(array))


def projected_columns(block, left, pieces, after):
    width, columns = block.shape
    part = width // pieces

    def kernel(block, left, after, out):
        for p in range(pieces):
            out[p] = lax.dot_general(
                block[...],
                left[:, pl.ds(p * part, part)],
                (((0,), (0,)), ((), ())),
                preferred_element_type=jnp.float32,
            ).astype(jnp.bfloat16)

    return pl.pallas_call(
        kernel,
        out_shape=jax.ShapeDtypeStruct((pieces, columns, part), jnp.bfloat16),
        in_specs=[pl.BlockSpec(memory_space=space) for space in (pltpu.VMEM, pltpu.VMEM, pl.ANY)],
        compiler_params=pltpu.CompilerParams(vmem_limit_bytes=16 * mib),
        cost_estimate=pl.CostEstimate(
            flops=2 * width * width * columns,
            bytes_accessed=2 * (width * width + 2 * width * columns),
            transcendentals=0,
        ),
    )(block, left, after)


def turned_step(projected, right, first_moment, second_moment):
    pieces, part, rows = projected.shape
    width = pieces * part

    def kernel(projected, right, first, second, back, direction):
        turned = projected[...].reshape(width, rows)
        cuts = [pl.ds(p * part, part) for p in range(pieces)]
        for cut in cuts:
            rotated = lax.dot_general(
                turned,
                right[:, cut],
                (((0,), (0,)), ((), ())),
                preferred_element_type=jnp.float32,
            )
            first_new = (
                beta_first * first[:, cut].astype(jnp.float32) + (1.0 - beta_first) * rotated
            )
            second_new = (
                beta_second * second[:, cut].astype(jnp.float32)
                + (1.0 - beta_second) * rotated * rotated
            )
            direction[:, cut] = (
                first_new / bias_first / (jnp.sqrt(second_new / bias_second) + epsilon)
            ).astype(jnp.bfloat16)
        for p, cut in enumerate(cuts):
            back[p] = lax.dot_general(
                direction[...],
                right[cut, :],
                (((1,), (1,)), ((), ())),
                preferred_element_type=jnp.float32,
            ).astype(jnp.bfloat16)

    return pl.pallas_call(
        kernel,
        out_shape=jax.ShapeDtypeStruct((pieces, rows, part), jnp.bfloat16),
        scratch_shapes=[pltpu.VMEM((rows, width), jnp.bfloat16)],
        compiler_params=pltpu.CompilerParams(vmem_limit_bytes=16 * mib),
        cost_estimate=pl.CostEstimate(
            flops=4 * rows * width * width,
            bytes_accessed=2 * (width * width + 4 * rows * width),
            transcendentals=2 * rows * width,
        ),
    )(projected, right, first_moment, second_moment)


def product(left, right):
    def kernel(left, right, out):
        out[...] = jnp.dot(
            left[...], right[...], preferred_element_type=jnp.float32
        ).astype(jnp.bfloat16)

    rows, inner = left.shape
    columns = right.shape[1]
    return pl.pallas_call(
        kernel,
        out_shape=jax.ShapeDtypeStruct((rows, columns), jnp.bfloat16),
        compiler_params=pltpu.CompilerParams(vmem_limit_bytes=16 * mib),
        cost_estimate=pl.CostEstimate(
            flops=2 * rows * inner * columns,
            bytes_accessed=2 * (rows * inner + inner * columns + rows * columns),
            transcendentals=0,
        ),
    )(left, right)


def taken(array, places):
    count = places.shape[0]
    shape = (count, *array.shape[1:])

    batch = max(n for n in range(1, 13) if count % n == 0)

    def kernel(places, source, target):
        def some(step, carry):
            first = step * batch
            rows = [source[places[first + n]] for n in range(batch)]
            for n, row in enumerate(rows):
                target[first + n] = row
            return carry

        lax.fori_loop(0, count // batch, some, 0)

    here = pl.BlockSpec(memory_space=pltpu.VMEM)
    return pl.pallas_call(
        kernel,
        out_shape=jax.ShapeDtypeStruct(shape, array.dtype),
        in_specs=[pl.BlockSpec(memory_space=pltpu.SMEM), here],
        out_specs=here,
        compiler_params=pltpu.CompilerParams(vmem_limit_bytes=8 * mib),
        cost_estimate=pl.CostEstimate(
            flops=0,
            bytes_accessed=2 * array.size * array.dtype.itemsize,
            transcendentals=0,
        ),
    )(places, array)


def local(grad_parts, owner_table, left_basis, right_basis, first_moment, second_moment):
    replicas, halves, depth = (lax.axis_size(axis) for axis in ("dp", "half", "z"))
    slots = halves * depth
    _, block_count, piece_rows, width = grad_parts.shape
    quarter = width // replicas
    left = left_basis[0]

    parts = exchange(cut_columns(grad_parts[0], replicas), "dp")
    summed = parts.astype(jnp.float32).sum(axis=0).astype(jnp.bfloat16)

    places = slot_places(owner_table, halves, depth)
    selector = (jnp.arange(cores * slots, dtype=jnp.int32)[:, None] == places[None, :]).astype(
        jnp.bfloat16
    )
    packed = jnp.dot(
        selector,
        summed.reshape(block_count, piece_rows * quarter),
        preferred_element_type=jnp.float32,
    ).astype(jnp.bfloat16)
    arrived = exchange(packed.reshape(cores, slots, piece_rows, quarter), "core")
    arrived, turn = in_turn(jnp.moveaxis(arrived, 1, 0), depth)
    block = exchange(arrived, ("half", "z"))

    projected = exchange(
        projected_columns(block.reshape(width, quarter), left, replicas, turn), "dp"
    )
    back = turned_step(projected, right_basis[0], first_moment[0], second_moment[0])
    back = exchange(back, "dp")
    update = product(left, back.reshape(width, quarter))

    returned = exchange(update.reshape(slots, cores, piece_rows, quarter), ("half", "z"))
    returned = exchange(jnp.moveaxis(returned, 1, 0), "core")
    return taken(returned.reshape(cores * slots, piece_rows, quarter), places)


def solution(mesh):
    replicas, halves, owners = (mesh.shape[axis] for axis in ("dp", "half", "own"))
    fine = Mesh(
        mesh.devices.reshape(replicas, halves, owners // cores, cores), ("dp", "half", "z", "core")
    )
    slots = ("half", "z", "core")
    return jax.shard_map(
        local,
        mesh=fine,
        in_specs=(
            P("dp", None, slots, None),
            P(),
            P(slots, None, None),
            P(slots, None, None),
            P(slots, "dp", None),
            P(slots, "dp", None),
        ),
        out_specs=P(None, slots, "dp"),
        check_vma=False,
    )
```

```python
import jax
import jax.numpy as jnp
from jax import lax
from jax.experimental import pallas as pl
from jax.experimental.pallas import tpu as pltpu
from jax.sharding import Mesh, PartitionSpec as P

beta_first = 0.9
beta_second = 0.95
bias_first = 1.0 - 0.9**10
bias_second = 1.0 - 0.95**10
epsilon = 1e-08
mib = 1 << 20
cores = 2


def in_hbm(array):
    return pltpu.with_memory_space_constraint(array, pltpu.HBM)


def exchange(array, axes):
    return lax.all_to_all(array, axes, split_axis=0, concat_axis=0, tiled=True)


def slot_places(owner_table, ranks, depth):
    owner_ids = owner_table[:, 0]
    positions = jnp.arange(owner_ids.shape[0], dtype=jnp.int32)
    shared = (owner_ids[:, None] == owner_ids[None, :]) & (positions[None, :] < positions[:, None])
    ranking = jnp.sum(shared.astype(jnp.int32), axis=1)
    return ((owner_ids % cores) * ranks + ranking) * depth + owner_ids // cores


def in_turn(array, halves, depth):
    def core_1(half, z):
        return (half % halves * depth + z % depth) * cores + 1

    pairs = [
        (core_1(half, z), core_1(half + halves // 2, z + depth // 2))
        for half in range(halves)
        for z in range(depth)
    ]
    turn = lax.ppermute(array[0, 0], ("half", "z", "core"), pairs)
    return lax.optimization_barrier((array, turn))


def cut_columns(array, pieces):
    blocks, rows, width = array.shape
    part = width // pieces

    steps = max(n for n in range(1, 5) if blocks % n == 0)
    some = blocks // steps

    def kernel(source, target, held, came, went):
        def arrival(n):
            return pltpu.make_async_copy(
                source.at[pl.ds(n * some, some)], held.at[pl.ds(n * some, some)], came.at[n]
            )

        def departure(n, p):
            return pltpu.make_async_copy(
                held.at[pl.ds(n * some, some), :, pl.ds(p * part, part)],
                target.at[p, pl.ds(n * some, some)],
                went.at[n, p],
            )

        for n in range(steps):
            arrival(n).start()
        for n in range(steps):
            arrival(n).wait()
            for p in range(pieces):
                departure(n, p).start()
        for n in range(steps):
            for p in range(pieces):
                departure(n, p).wait()

    return pl.pallas_call(
        kernel,
        out_shape=jax.ShapeDtypeStruct((pieces, blocks, rows, part), array.dtype),
        in_specs=[pl.BlockSpec(memory_space=pltpu.HBM)],
        out_specs=pl.BlockSpec(memory_space=pl.ANY),
        scratch_shapes=[
            pltpu.VMEM(array.shape, array.dtype),
            pltpu.SemaphoreType.DMA((steps,)),
            pltpu.SemaphoreType.DMA((steps, pieces)),
        ],
        compiler_params=pltpu.CompilerParams(vmem_limit_bytes=8 * mib),
        cost_estimate=pl.CostEstimate(
            flops=0, bytes_accessed=2 * array.size * array.dtype.itemsize, transcendentals=0
        ),
    )(in_hbm(array))


def projected_columns(block, left, pieces, after):
    width, columns = block.shape
    part = width // pieces

    def kernel(block, left, after, out):
        for p in range(pieces):
            out[p] = lax.dot_general(
                block[...],
                left[:, pl.ds(p * part, part)],
                (((0,), (0,)), ((), ())),
                preferred_element_type=jnp.float32,
            ).astype(jnp.bfloat16)

    return pl.pallas_call(
        kernel,
        out_shape=jax.ShapeDtypeStruct((pieces, columns, part), jnp.bfloat16),
        in_specs=[pl.BlockSpec(memory_space=space) for space in (pltpu.VMEM, pltpu.VMEM, pl.ANY)],
        compiler_params=pltpu.CompilerParams(vmem_limit_bytes=16 * mib),
        cost_estimate=pl.CostEstimate(
            flops=2 * width * width * columns,
            bytes_accessed=2 * (width * width + 2 * width * columns),
            transcendentals=0,
        ),
    )(block, left, after)


def turned_step(projected, right, first_moment, second_moment):
    pieces, part, rows = projected.shape
    width = pieces * part

    def kernel(projected, right, first, second, back, direction):
        turned = projected[...].reshape(width, rows)
        cuts = [pl.ds(p * part, part) for p in range(pieces)]
        for cut in cuts:
            rotated = lax.dot_general(
                turned,
                right[:, cut],
                (((0,), (0,)), ((), ())),
                preferred_element_type=jnp.float32,
            )
            first_new = (
                beta_first * first[:, cut].astype(jnp.float32) + (1.0 - beta_first) * rotated
            )
            second_new = (
                beta_second * second[:, cut].astype(jnp.float32)
                + (1.0 - beta_second) * rotated * rotated
            )
            direction[:, cut] = (
                first_new / bias_first / (jnp.sqrt(second_new / bias_second) + epsilon)
            ).astype(jnp.bfloat16)
        for p, cut in enumerate(cuts):
            back[p] = lax.dot_general(
                direction[...],
                right[cut, :],
                (((1,), (1,)), ((), ())),
                preferred_element_type=jnp.float32,
            ).astype(jnp.bfloat16)

    return pl.pallas_call(
        kernel,
        out_shape=jax.ShapeDtypeStruct((pieces, rows, part), jnp.bfloat16),
        scratch_shapes=[pltpu.VMEM((rows, width), jnp.bfloat16)],
        compiler_params=pltpu.CompilerParams(vmem_limit_bytes=16 * mib),
        cost_estimate=pl.CostEstimate(
            flops=4 * rows * width * width,
            bytes_accessed=2 * (width * width + 4 * rows * width),
            transcendentals=2 * rows * width,
        ),
    )(projected, right, first_moment, second_moment)


def product(left, right):
    def kernel(left, right, out):
        out[...] = jnp.dot(
            left[...], right[...], preferred_element_type=jnp.float32
        ).astype(jnp.bfloat16)

    rows, inner = left.shape
    columns = right.shape[1]
    return pl.pallas_call(
        kernel,
        out_shape=jax.ShapeDtypeStruct((rows, columns), jnp.bfloat16),
        compiler_params=pltpu.CompilerParams(vmem_limit_bytes=16 * mib),
        cost_estimate=pl.CostEstimate(
            flops=2 * rows * inner * columns,
            bytes_accessed=2 * (rows * inner + inner * columns + rows * columns),
            transcendentals=0,
        ),
    )(left, right)


def taken(array, places):
    count = places.shape[0]
    shape = (count, *array.shape[1:])

    batch = max(n for n in range(1, 13) if count % n == 0)

    def kernel(places, source, target):
        def some(step, carry):
            first = step * batch
            rows = [source[places[first + n]] for n in range(batch)]
            for n, row in enumerate(rows):
                target[first + n] = row
            return carry

        lax.fori_loop(0, count // batch, some, 0)

    here = pl.BlockSpec(memory_space=pltpu.VMEM)
    return pl.pallas_call(
        kernel,
        out_shape=jax.ShapeDtypeStruct(shape, array.dtype),
        in_specs=[pl.BlockSpec(memory_space=pltpu.SMEM), here],
        out_specs=here,
        compiler_params=pltpu.CompilerParams(vmem_limit_bytes=8 * mib),
        cost_estimate=pl.CostEstimate(
            flops=0,
            bytes_accessed=2 * array.size * array.dtype.itemsize,
            transcendentals=0,
        ),
    )(places, array)


def local(grad_parts, owner_table, left_basis, right_basis, first_moment, second_moment):
    replicas, halves, depth = (lax.axis_size(axis) for axis in ("dp", "half", "z"))
    slots = halves * depth
    _, block_count, piece_rows, width = grad_parts.shape
    quarter = width // replicas
    left = left_basis[0]

    parts = exchange(cut_columns(grad_parts[0], replicas), "dp")
    summed = parts.astype(jnp.float32).sum(axis=0).astype(jnp.bfloat16)

    places = slot_places(owner_table, halves, depth)
    selector = (jnp.arange(cores * slots, dtype=jnp.int32)[:, None] == places[None, :]).astype(
        jnp.bfloat16
    )
    packed = jnp.dot(
        selector,
        summed.reshape(block_count, piece_rows * quarter),
        preferred_element_type=jnp.float32,
    ).astype(jnp.bfloat16)
    arrived = exchange(packed.reshape(cores, slots, piece_rows, quarter), "core")
    arrived, turn = in_turn(jnp.moveaxis(arrived, 1, 0), halves, depth)
    block = exchange(arrived, ("half", "z"))

    projected = exchange(
        projected_columns(block.reshape(width, quarter), left, replicas, turn), "dp"
    )
    back = turned_step(projected, right_basis[0], first_moment[0], second_moment[0])
    back = exchange(back, "dp")
    update = product(left, back.reshape(width, quarter))

    returned = exchange(update.reshape(slots, cores, piece_rows, quarter), ("half", "z"))
    returned = exchange(jnp.moveaxis(returned, 1, 0), "core")
    return taken(returned.reshape(cores * slots, piece_rows, quarter), places)


def solution(mesh):
    replicas, halves, owners = (mesh.shape[axis] for axis in ("dp", "half", "own"))
    fine = Mesh(
        mesh.devices.reshape(replicas, halves, owners // cores, cores), ("dp", "half", "z", "core")
    )
    slots = ("half", "z", "core")
    return jax.shard_map(
        local,
        mesh=fine,
        in_specs=(
            P("dp", None, slots, None),
            P(),
            P(slots, None, None),
            P(slots, None, None),
            P(slots, "dp", None),
            P(slots, "dp", None),
        ),
        out_specs=P(None, slots, "dp"),
        check_vma=False,
    )
```
